32 devices in a mesh: group: 2 (over x), expert: 16 (over z, y, core).
Axes of the slice: x: 2, y: 2, z: 4, core: 2. Of those that a mesh axis runs over, the one named last changes fastest.
Arguments:
- tokens: bfloat16 [4096, 2048], P(('group', 'expert')), may hold values from -6 to 6
- cotangent: bfloat16 [4096, 2048], P(('group', 'expert')), may hold values from -6 to 6
- gate_probs: float32 [4096, 8], P(('group', 'expert')), may hold values from 0.02 to 0.5
- expert_ids: int32 [4096, 8], P(('group', 'expert')), may hold values from 0 to 15, all different within a row; in each aligned block of 128 rows (0 to 127, 128 to 255, ...) at most 128 rows name the same one
- gate_up: bfloat16 [16, 2048, 768], P('expert'), may hold values from -0.125 to 0.125
- down_weight: bfloat16 [16, 384, 2048], P('expert'), may hold values from -0.3125 to 0.3125
- gate_up_moment: float32 [16, 2048, 768], P('expert', 'group'), may hold values from -6 to 6
- gate_up_second: float32 [16, 2048, 768], P('expert', 'group'), may hold values from 0.05 to 20
- down_moment: float32 [16, 384, 2048], P('expert', None, 'group'), may hold values from -6 to 6
- down_second: float32 [16, 384, 2048], P('expert', None, 'group'), may hold values from 0.05 to 20
Outputs:
- token_grad: bfloat16 [4096, 2048], P(('group', 'expert'))
- updated_gate_up: bfloat16 [16, 2048, 768], P('expert')
- updated_down: bfloat16 [16, 384, 2048], P('expert')
- gate_up_moment_out: float32 [16, 2048, 768], P('expert', 'group')
- gate_up_second_out: float32 [16, 2048, 768], P('expert', 'group')
- down_moment_out: float32 [16, 384, 2048], P('expert', None, 'group')
- down_second_out: float32 [16, 384, 2048], P('expert', None, 'group')
The draws below stay inside these ranges and needn't reach their ends.
Inputs may be any that keep to these rules, and one draw needn't show every extreme that they name: `expert_ids`: each row names 8 different experts. In the rows of one device no expert is named by more than 128 rows, and in every draw some expert is named by exactly 128 rows of some device.
All inputs are finite; a program needn't handle non-finite values.
Results may differ from the reference program's by a relative error of at most 0.015.
Values may be sent and summed in bfloat16 or wider, within the bound.
A program may use at most 192 MiB of HBM per device.

```python
import math
import jax
import jax.numpy as jnp
import numpy as np
from jax import lax

D = 2048
HIDDEN_SIZE = 384
TOP = 8
TOK_DEV = 128
EXPERTS = 16
CAP = 128
TOKENS = 4096
N_GROUP = 2
N_EXPERT = 16


def levels(own_key, extent, pieces, low, largest):
    def one(position, blocks):
        draws = jax.random.uniform(jax.random.fold_in(jax.random.fold_in(own_key, 6), position), (blocks,), jnp.float32, low / len(pieces), largest / len(pieces))
        return jnp.repeat(jnp.exp(draws), extent[position] // blocks).reshape((-1,) + (1,) * (len(extent) - position - 1))

    level = one(*pieces[0])
    for cut in pieces[1:]:
        level = level * one(*cut)
    return level


def routed_block(key, own, number, rows, number_of, top, limit, lean):
    order = jax.random.permutation(key, number_of)
    crowded, common = load_shares(number_of, rows * top, limit, lean, True), load_shares(number_of, rows * top, limit, lean, False)
    places = jnp.arange(number_of)

    def named(sizes, offset_by):
        used = int((sizes > 0).sum())
        fixed = max(1, used // 4)
        passed = fixed + (places - fixed + offset_by * (used - fixed)) % max(1, number_of - fixed)
        return jnp.zeros((number_of,), jnp.int32).at[order[jnp.where(places < fixed, places, passed)]].set(jnp.asarray(sizes, jnp.int32))

    sizes = jnp.where(number % 4 == 0, named(crowded, number // 4), named(common, number - number // 4 - 1))
    mixed = jax.random.permutation(jax.random.fold_in(own, 3), number_of)
    donor, receiver = mixed[0:number_of // 2 * 2:2], mixed[1:number_of // 2 * 2:2]
    room = jnp.minimum(sizes[donor] - 1, limit - sizes[receiver]) // 2
    room = jnp.where((donor == order[0]) | (receiver == order[0]) | (sizes[receiver] == 0), 0, jnp.maximum(room, 0))
    passed = jax.random.randint(jax.random.fold_in(own, 4), (number_of // 2,), 0, 1 << 20) % (room + 1)
    sizes = sizes.at[donor].add(-passed).at[receiver].add(passed)
    members = jnp.searchsorted(jnp.cumsum(sizes), jnp.arange(rows * top), side="right").astype(jnp.int32)
    listing = members.reshape(top, rows).T
    listing = listing[jax.random.permutation(jax.random.fold_in(own, 1), rows)]
    offset_by = jax.random.randint(jax.random.fold_in(own, 2), (rows, 1), 0, top)
    return jnp.take_along_axis(listing, (jnp.arange(top)[None, :] + offset_by) % top, axis=1)


def load_shares(amount, total, reach, skew, full):
    weights = [(1 << 20) // math.isqrt(standing ** skew) + 1 for standing in range(1, amount + 1)]
    largest = reach if full else min(reach, max(-(-total // amount), total * weights[0] // sum(weights)))
    least = 1 if total - largest >= amount - 1 else 0
    holding, surplus = [largest] + [least] * (amount - 1), total - largest - least * (amount - 1)
    while surplus > 0:
        free = [i for i in range(1, amount) if holding[i] < largest] or [i for i in range(1, amount) if holding[i] < reach]
        pool, left = sum([weights[i] for i in free]), surplus
        for i in free:
            more = min(reach - holding[i], max(1, left * weights[i] // pool), surplus)
            holding[i] = holding[i] + more
            surplus = surplus - more
    return np.array(holding)


def scatter_about(own_key, extent, width, limit, pieces=(), kind=jnp.bfloat16):
    result = jax.random.normal(own_key, extent, jnp.float32) * width
    if len(pieces) > 0:
        result = levels(own_key, extent, pieces, -0.22, 0.18) * result
    return jnp.clip(result, min=-limit, max=limit).astype(kind)


def setup_inputs(seed: int = 0) -> dict:
    splits = jax.random.split(jax.random.key(seed), 11)
    tokens = scatter_about(splits[0], (TOKENS, D), 1.0, 6.0, ((0, 32),))
    cotangent = scatter_about(splits[1], (TOKENS, D), 1.0, 6.0, ((0, 32),))
    gate_probs = jnp.clip(jnp.exp(math.log(0.5) - 3.218876 * jax.random.uniform(splits[2], (TOKENS, TOP), jnp.float32) ** levels(splits[2], (TOKENS, TOP), ((0, 32),), -0.2, 0.2)), 0.02, 0.5)
    expert_ids_keys = jax.random.split(jax.random.fold_in(splits[3], 1), TOKENS // TOK_DEV)
    expert_ids_turns = jax.random.permutation(jax.random.fold_in(splits[3], 3), TOKENS // TOK_DEV)
    expert_ids = jax.vmap(lambda own, number: routed_block(jax.random.fold_in(splits[3], 2), own, number, TOK_DEV, EXPERTS, TOP, CAP, 1))(expert_ids_keys, expert_ids_turns).reshape((TOKENS, TOP))
    gate_up = scatter_about(splits[4], (EXPERTS, D, 2 * HIDDEN_SIZE), D ** -0.5, 0.125, ((0, 16),))
    down_weight = scatter_about(splits[5], (EXPERTS, HIDDEN_SIZE, D), HIDDEN_SIZE ** -0.5, 0.3125, ((0, 16),))
    gate_up_moment = scatter_about(splits[6], (EXPERTS, D, 2 * HIDDEN_SIZE), 1.0, 6.0, ((0, 16), (1, 2)), jnp.float32)
    gate_up_second = jnp.clip(jnp.exp(math.log(20.0) - 5.9914645 * jax.random.uniform(splits[7], (EXPERTS, D, 2 * HIDDEN_SIZE), jnp.float32) ** levels(splits[7], (EXPERTS, D, 2 * HIDDEN_SIZE), ((0, 16), (1, 2)), -0.2, 0.2)), 0.05, 20.0)
    down_moment = scatter_about(splits[8], (EXPERTS, HIDDEN_SIZE, D), 1.0, 6.0, ((0, 16), (2, 2)), jnp.float32)
    down_second = jnp.clip(jnp.exp(math.log(20.0) - 5.9914645 * jax.random.uniform(splits[9], (EXPERTS, HIDDEN_SIZE, D), jnp.float32) ** levels(splits[9], (EXPERTS, HIDDEN_SIZE, D), ((0, 16), (2, 2)), -0.2, 0.2)), 0.05, 20.0)
    return dict(tokens=tokens, cotangent=cotangent, gate_probs=gate_probs, expert_ids=expert_ids, gate_up=gate_up, down_weight=down_weight, gate_up_moment=gate_up_moment, gate_up_second=gate_up_second, down_moment=down_moment, down_second=down_second)


learn_rate = 0.001
beta_first = 0.9
beta_second = 0.999
adam_eps = 1e-08

def expert_backward(inputs, scaled_grad, weight_gate_up, weight_down):
    hidden_count = weight_down.shape[0]
    projected = jnp.dot(inputs, weight_gate_up, preferred_element_type=jnp.float32)
    gate_part = projected[:, :hidden_count]
    up_part = projected[:, hidden_count:]
    sigmoid_gate = jax.nn.sigmoid(gate_part)
    activated = gate_part * sigmoid_gate
    hidden_act = (activated * up_part).astype(jnp.bfloat16)
    hidden_grad = jnp.dot(scaled_grad, weight_down.T, preferred_element_type=jnp.float32)
    slope = sigmoid_gate * (1.0 + gate_part * (1.0 - sigmoid_gate))
    pair_grad = jnp.concatenate([hidden_grad * up_part * slope, hidden_grad * activated], axis=1).astype(jnp.bfloat16)
    down_grad = jnp.dot(hidden_act.T, scaled_grad, preferred_element_type=jnp.float32)
    gate_up_grad = jnp.dot(inputs.T, pair_grad, preferred_element_type=jnp.float32)
    input_grad = jnp.dot(pair_grad, weight_gate_up.T, preferred_element_type=jnp.float32).astype(jnp.bfloat16)
    return (gate_up_grad, down_grad, input_grad)

def adam_update(weight, grad, first, second):
    first_new = beta_first * first + (1.0 - beta_first) * grad
    second_new = beta_second * second + (1.0 - beta_second) * grad * grad
    updated = (weight.astype(jnp.float32) - learn_rate * first_new / (jnp.sqrt(second_new) + adam_eps)).astype(jnp.bfloat16)
    return (updated, first_new, second_new)

def reference(tokens, cotangent, gate_probs, expert_ids, gate_up, down_weight, gate_up_moment, gate_up_second, down_moment, down_second):
    devices = N_GROUP * N_EXPERT
    per_device = TOK_DEV * TOP
    flat_ids = expert_ids.reshape(devices, per_device)
    onehot = (flat_ids[:, :, None] == jnp.arange(EXPERTS, dtype=jnp.int32)[None, None, :]).astype(jnp.int32)
    before = jnp.cumsum(onehot, axis=1) - onehot
    slot_rank = lax.optimization_barrier(jnp.sum(before * onehot, axis=2)).astype(jnp.int32)
    slot_index = (flat_ids * CAP + slot_rank).astype(jnp.int32)
    source_rows = jnp.broadcast_to(jnp.arange(devices, dtype=jnp.int32)[:, None], (devices, per_device))
    pair_ids = jnp.broadcast_to(jnp.arange(per_device, dtype=jnp.int32)[None, :], (devices, per_device))
    table = jnp.full((devices, EXPERTS * CAP), -1, jnp.int32).at[source_rows, slot_index].set(pair_ids)
    table = table.reshape(devices, EXPERTS, CAP)
    owners = jnp.repeat(jnp.arange(devices, dtype=jnp.int32), CAP)

    def per_expert(accum, expert_index):
        entries = lax.dynamic_index_in_dim(table, expert_index, 1, keepdims=False).reshape(-1)
        usable = entries >= 0
        clamped = jnp.where(usable, entries, 0).astype(jnp.int32)
        token_index = (owners * TOK_DEV + clamped // TOP).astype(jnp.int32)
        pick_index = (clamped % TOP).astype(jnp.int32)
        inputs = jnp.where(usable[:, None], tokens[token_index], jnp.zeros((), jnp.bfloat16))
        weights = jnp.where(usable, gate_probs[token_index, pick_index], jnp.zeros((), jnp.float32))
        scaled = (weights[:, None] * cotangent[token_index].astype(jnp.float32)).astype(jnp.bfloat16)
        grad_pair, grad_down, input_grad = expert_backward(inputs, scaled, gate_up[expert_index], down_weight[expert_index])
        accum = accum.at[token_index].add(jnp.where(usable[:, None], input_grad.astype(jnp.float32), jnp.zeros((), jnp.float32)))
        return (accum, (grad_pair, grad_down))
    start = jnp.zeros((TOKENS, D), jnp.float32)
    accum, grads = lax.scan(per_expert, start, jnp.arange(EXPERTS, dtype=jnp.int32))
    grad_pair, grad_down = grads
    new_gate_up, first_gate_up, second_gate_up = adam_update(gate_up, grad_pair, gate_up_moment, gate_up_second)
    new_down, first_down, second_down = adam_update(down_weight, grad_down, down_moment, down_second)
    return (accum.astype(jnp.bfloat16), new_gate_up, new_down, first_gate_up, second_gate_up, first_down, second_down)
```

```python
import jax
import jax.numpy as jnp
from jax import lax
from jax.sharding import PartitionSpec as P

learn_rate = 0.001
beta_first = 0.9
beta_second = 0.999
adam_eps = 1e-08


def adam_update(weight, grad, first, second):
    first_new = beta_first * first + (1.0 - beta_first) * grad
    second_new = beta_second * second + (1.0 - beta_second) * grad * grad
    updated = (
        weight.astype(jnp.float32) - learn_rate * first_new / (jnp.sqrt(second_new) + adam_eps)
    ).astype(jnp.bfloat16)
    return (updated, first_new, second_new)


def contract(a, b, dims):
    return lax.dot_general(a, b, (dims, ((), ())), preferred_element_type=jnp.float32)


def local(
    tokens,
    cotangent,
    gate_probs,
    expert_ids,
    gate_up,
    down_weight,
    gate_up_moment,
    gate_up_second,
    down_moment,
    down_second,
):
    expert_count = lax.axis_size("expert")
    model_width = tokens.shape[1]
    me = lax.axis_index("expert")
    experts = jnp.arange(expert_count, dtype=jnp.int32)
    dense = jnp.sum(
        jnp.where(expert_ids[:, :, None] == experts, gate_probs[:, :, None], 0.0), axis=1
    )
    weights = lax.all_gather(dense, "expert", axis=0, tiled=True)
    weight = lax.dynamic_slice_in_dim(weights, me, 1, 1)
    all_tokens = lax.all_gather(tokens, "expert", axis=0, tiled=True)
    all_cotangent = lax.all_gather(cotangent, "expert", axis=0, tiled=True)
    weight_pair = gate_up[0]
    weight_down = down_weight[0]
    hidden_count = weight_down.shape[0]
    projected = contract(all_tokens, weight_pair, ((1,), (0,)))
    gate_part = projected[:, :hidden_count]
    up_part = projected[:, hidden_count:]
    sigmoid_gate = jax.nn.sigmoid(gate_part)
    activated = gate_part * sigmoid_gate
    hidden_act = (weight * activated * up_part).astype(jnp.bfloat16)
    hidden_grad = weight * contract(all_cotangent, weight_down, ((1,), (1,)))
    slope = sigmoid_gate * (1.0 + gate_part * (1.0 - sigmoid_gate))
    pair_grad = jnp.concatenate(
        [hidden_grad * up_part * slope, hidden_grad * activated], axis=1
    ).astype(jnp.bfloat16)
    grad_pair = contract(all_tokens, pair_grad, ((0,), (0,))).astype(jnp.bfloat16)
    sum_pair = lax.psum_scatter(grad_pair[None], "group", scatter_dimension=1, tiled=True)
    row_grads = contract(pair_grad, weight_pair, ((1,), (1,))).astype(jnp.bfloat16)
    token_grad = lax.psum_scatter(row_grads, "expert", scatter_dimension=0, tiled=True)
    grad_down = contract(hidden_act, all_cotangent, ((0,), (0,))).astype(jnp.bfloat16)
    sum_down = lax.psum_scatter(grad_down[None], "group", scatter_dimension=2, tiled=True)
    group_index = lax.axis_index("group")
    share_rows = model_width // lax.axis_size("group")
    own_pair = lax.dynamic_slice_in_dim(gate_up, group_index * share_rows, share_rows, 1)
    own_down = lax.dynamic_slice_in_dim(down_weight, group_index * share_rows, share_rows, 2)
    new_pair, first_pair, second_pair = adam_update(
        own_pair, sum_pair.astype(jnp.float32), gate_up_moment, gate_up_second
    )
    new_down, first_down, second_down = adam_update(
        own_down, sum_down.astype(jnp.float32), down_moment, down_second
    )
    full_pair = lax.all_gather(new_pair, "group", axis=1, tiled=True)
    full_down = lax.all_gather(new_down, "group", axis=2, tiled=True)
    return (token_grad, full_pair, full_down, first_pair, second_pair, first_down, second_down)


def solution(mesh):
    placed = (
        P(("group", "expert"), None),
        P(("group", "expert"), None),
        P(("group", "expert"), None),
        P(("group", "expert"), None),
        P("expert", None, None),
        P("expert", None, None),
        P("expert", "group", None),
        P("expert", "group", None),
        P("expert", None, "group"),
        P("expert", None, "group"),
    )
    return jax.shard_map(
        local,
        mesh=mesh,
        in_specs=placed,
        out_specs=(
            P(("group", "expert"), None),
            P("expert", None, None),
            P("expert", None, None),
            P("expert", "group", None),
            P("expert", "group", None),
            P("expert", None, "group"),
            P("expert", None, "group"),
        ),
        check_vma=False,
    )
```

```python
import jax
import jax.numpy as jnp
from jax import lax
from jax.sharding import PartitionSpec as P

learn_rate = 0.001
beta_first = 0.9
beta_second = 0.999
adam_eps = 1e-08


def adam_update(weight, grad, first, second):
    first_new = beta_first * first + (1.0 - beta_first) * grad
    second_new = beta_second * second + (1.0 - beta_second) * grad * grad
    updated = (
        weight.astype(jnp.float32) - learn_rate * first_new / (jnp.sqrt(second_new) + adam_eps)
    ).astype(jnp.bfloat16)
    return (updated, first_new, second_new)


def contract(a, b, dims):
    return lax.dot_general(a, b, (dims, ((), ())), preferred_element_type=jnp.float32)


def group_reduce(partial, dim):
    size = lax.axis_size("group")
    share = partial.shape[dim] // size
    own = lax.axis_index("group")
    total = lax.dynamic_slice_in_dim(partial, own * share, share, dim)
    for step in range(1, size):
        sent = lax.dynamic_slice_in_dim(partial, (own + step) % size * share, share, dim)
        pairs = [(i, (i + step) % size) for i in range(size)]
        total = total + lax.ppermute(sent.astype(jnp.bfloat16), "group", pairs).astype(jnp.float32)
    return total


def group_gather(block, dim):
    size = lax.axis_size("group")
    share = block.shape[dim]
    own = lax.axis_index("group")
    whole = jnp.zeros(block.shape[:dim] + (share * size,) + block.shape[dim + 1 :], block.dtype)
    whole = lax.dynamic_update_slice_in_dim(whole, block, own * share, dim)
    for step in range(1, size):
        pairs = [(i, (i + step) % size) for i in range(size)]
        came = lax.ppermute(block, "group", pairs)
        whole = lax.dynamic_update_slice_in_dim(whole, came, (own - step) % size * share, dim)
    return whole


def local(
    tokens,
    cotangent,
    gate_probs,
    expert_ids,
    gate_up,
    down_weight,
    gate_up_moment,
    gate_up_second,
    down_moment,
    down_second,
):
    expert_count = lax.axis_size("expert")
    model_width = tokens.shape[1]
    me = lax.axis_index("expert")
    experts = jnp.arange(expert_count, dtype=jnp.int32)
    dense = jnp.sum(
        jnp.where(expert_ids[:, :, None] == experts, gate_probs[:, :, None], 0.0), axis=1
    )
    high = dense.astype(jnp.bfloat16)
    low = (dense - high.astype(jnp.float32)).astype(jnp.bfloat16)
    pad = -2 * expert_count % 128
    side = jnp.concatenate([high, low, jnp.zeros((tokens.shape[0], pad), jnp.bfloat16)], axis=1)
    all_tokens = lax.all_gather(tokens, "expert", axis=0, tiled=True)
    gathered = lax.all_gather(
        jnp.concatenate([cotangent, side], axis=1), "expert", axis=0, tiled=True
    )
    all_cotangent = gathered[:, :model_width]
    weight = sum(
        lax.dynamic_slice_in_dim(gathered, model_width + part * expert_count + me, 1, 1).astype(
            jnp.float32
        )
        for part in range(2)
    )
    weight_pair = gate_up[0]
    weight_down = down_weight[0]
    hidden_count = weight_down.shape[0]
    projected = contract(all_tokens, weight_pair, ((1,), (0,)))
    gate_part = projected[:, :hidden_count]
    up_part = projected[:, hidden_count:]
    sigmoid_gate = jax.nn.sigmoid(gate_part)
    activated = gate_part * sigmoid_gate
    hidden_act = (weight * activated * up_part).astype(jnp.bfloat16)
    hidden_grad = weight * contract(all_cotangent, weight_down, ((1,), (1,)))
    slope = sigmoid_gate * (1.0 + gate_part * (1.0 - sigmoid_gate))
    pair_grad = jnp.concatenate(
        [hidden_grad * up_part * slope, hidden_grad * activated], axis=1
    ).astype(jnp.bfloat16)
    row_grads = contract(pair_grad, weight_pair, ((1,), (1,))).astype(jnp.bfloat16)
    row_grads, pair_grad = lax.optimization_barrier((row_grads, pair_grad))
    token_grad = lax.psum_scatter(row_grads, "expert", scatter_dimension=0, tiled=True)
    grad_pair = contract(all_tokens, pair_grad, ((0,), (0,)))
    sum_pair = group_reduce(grad_pair, 0)[None]
    grad_down = contract(hidden_act, all_cotangent, ((0,), (0,)))
    sum_down = group_reduce(grad_down, 1)[None]
    group_index = lax.axis_index("group")
    share_rows = model_width // lax.axis_size("group")
    own_pair = lax.dynamic_slice_in_dim(gate_up, group_index * share_rows, share_rows, 1)
    own_down = lax.dynamic_slice_in_dim(down_weight, group_index * share_rows, share_rows, 2)
    new_pair, first_pair, second_pair = adam_update(
        own_pair, sum_pair, gate_up_moment, gate_up_second
    )
    new_down, first_down, second_down = adam_update(
        own_down, sum_down, down_moment, down_second
    )
    full_pair = group_gather(new_pair, 1)
    full_down = group_gather(new_down, 2)
    return (token_grad, full_pair, full_down, first_pair, second_pair, first_down, second_down)


def solution(mesh):
    placed = (
        P(("group", "expert"), None),
        P(("group", "expert"), None),
        P(("group", "expert"), None),
        P(("group", "expert"), None),
        P("expert", None, None),
        P("expert", None, None),
        P("expert", "group", None),
        P("expert", "group", None),
        P("expert", None, "group"),
        P("expert", None, "group"),
    )
    return jax.shard_map(
        local,
        mesh=mesh,
        in_specs=placed,
        out_specs=(
            P(("group", "expert"), None),
            P("expert", None, None),
            P("expert", None, None),
            P("expert", "group", None),
            P("expert", "group", None),
            P("expert", None, "group"),
            P("expert", None, "group"),
        ),
        check_vma=False,
    )
```

```python
import functools

import jax
import jax.numpy as jnp
from jax import lax
from jax.experimental import pallas as pl
from jax.experimental.pallas import tpu as pltpu
from jax.sharding import PartitionSpec as P

learn_rate = 0.001
beta_first = 0.9
beta_second = 0.999
adam_eps = 1e-08


def adam_update(weight, grad, first, second):
    first_new = beta_first * first + (1.0 - beta_first) * grad
    second_new = beta_second * second + (1.0 - beta_second) * grad * grad
    updated = (
        weight.astype(jnp.float32) - learn_rate * first_new / (jnp.sqrt(second_new) + adam_eps)
    ).astype(jnp.bfloat16)
    return (updated, first_new, second_new)


def contract(a, b, dims):
    return lax.dot_general(a, b, (dims, ((), ())), preferred_element_type=jnp.float32)


def group_reduce(partial, dim):
    size = lax.axis_size("group")
    share = partial.shape[dim] // size
    own = lax.axis_index("group")
    total = lax.dynamic_slice_in_dim(partial, own * share, share, dim)
    for step in range(1, size):
        sent = lax.dynamic_slice_in_dim(partial, (own + step) % size * share, share, dim)
        pairs = [(i, (i + step) % size) for i in range(size)]
        total = total + lax.ppermute(sent.astype(jnp.bfloat16), "group", pairs).astype(jnp.float32)
    return total


def group_gather(block, dim):
    size = lax.axis_size("group")
    share = block.shape[dim]
    own = lax.axis_index("group")
    whole = jnp.zeros(block.shape[:dim] + (share * size,) + block.shape[dim + 1 :], block.dtype)
    whole = lax.dynamic_update_slice_in_dim(whole, block, own * share, dim)
    for step in range(1, size):
        pairs = [(i, (i + step) % size) for i in range(size)]
        came = lax.ppermute(block, "group", pairs)
        whole = lax.dynamic_update_slice_in_dim(whole, came, (own - step) % size * share, dim)
    return whole


LINE = 4
CORES = 2


def gather_kernel(size, first_ref, second_ref, first_out, second_out, send_sem, recv_sem, own_sem):
    rows = size // (LINE * CORES)
    me = lax.axis_index("expert")
    core = me % CORES
    col = me // CORES % rows
    line = me // (CORES * rows)
    sources, outs = (first_ref, second_ref), (first_out, second_out)

    def device(at_line, at_col, at_core):
        return (at_line * rows + at_col) * CORES + at_core

    steps = {
        "up": (line < LINE - 1, device(line + 1, col, core)),
        "down": (line > 0, device(line - 1, col, core)),
        "right": (col < rows - 1, device(line, col + 1, core)),
        "left": (col > 0, device(line, col - 1, core)),
        "sibling": (core >= 0, device(line, col, 1 - core)),
    }

    barrier = pltpu.get_barrier_semaphore()
    for exists, target in steps.values():
        @pl.when(exists)
        def _(target=target):
            pl.semaphore_signal(
                barrier, inc=1, device_id={"expert": target}, device_id_type=pl.DeviceIdType.MESH
            )
    count = 1
    for name in ("up", "down", "right", "left"):
        count = count + jnp.where(steps[name][0], 1, 0)
    pl.semaphore_wait(barrier, count)

    sends = []

    def copy(kind, block, target, sem, src):
        return pltpu.make_async_remote_copy(
            src_ref=src,
            dst_ref=outs[kind].at[block],
            send_sem=send_sem.at[sem],
            recv_sem=recv_sem.at[kind, block],
            device_id={"expert": target},
            device_id_type=pl.DeviceIdType.MESH,
        )

    def forward(kind, block, valid, names, src=None):
        for name in names:
            exists, target = steps[name]
            sem = len(sends)
            sends.append((valid & exists, kind, block, target, sem, src))

            @pl.when(valid & exists)
            def _():
                copy(kind, block, target, sem, outs[kind].at[block] if src is None else src).start()

    def arrive(kind, block, valid):
        @pl.when(valid)
        def _():
            copy(kind, block, steps["sibling"][1], 0, outs[kind].at[block]).wait_recv()

    always = core >= 0
    for kind in range(2):
        forward(
            kind, me, always, ("right", "left", "up", "down", "sibling"), sources[kind]
        )
    for kind in range(2):
        pltpu.make_async_copy(sources[kind], outs[kind].at[me], own_sem.at[kind]).start()
    lanes = [(line, always)]
    for far in range(1, LINE):
        for kind in range(2):
            for at_line, valid, onward in (
                (line - far, line >= far, "up"),
                (line + far, line < LINE - far, "down"),
            ):
                block = device(at_line, col, core)
                arrive(kind, block, valid)
                forward(kind, block, valid, ("right", "left", onward, "sibling"))
        lanes += [(line - far, line >= far), (line + far, line < LINE - far)]
    for far in range(1, rows):
        for at_line, valid in lanes:
            for kind in range(2):
                for at_col, within, onward in (
                    (col - far, col >= far, "right"),
                    (col + far, col < rows - far, "left"),
                ):
                    block = device(at_line, at_col, core)
                    arrive(kind, block, valid & within)
                    forward(kind, block, valid & within, (onward, "sibling"))
    for at_line in range(LINE):
        for at_col in range(rows):
            for kind in range(2):
                arrive(kind, device(at_line, at_col, 1 - core), always)
    for kind in range(2):
        pltpu.make_async_copy(sources[kind], outs[kind].at[me], own_sem.at[kind]).wait()
    for valid, kind, block, target, sem, src in sends:
        @pl.when(valid)
        def _():
            copy(kind, block, target, sem, outs[kind].at[block] if src is None else src).wait_send()


def gather_pair(first, second):
    size = lax.axis_size("expert")
    rows = size // (LINE * CORES)
    send_count = 2 * (5 + 8 * (LINE - 1) + 4 * (rows - 1) * (2 * LINE - 1))
    outs = pl.pallas_call(
        functools.partial(gather_kernel, size),
        out_shape=[jax.ShapeDtypeStruct((size,) + x.shape, x.dtype) for x in (first, second)],
        in_specs=[pl.BlockSpec(memory_space=pl.ANY)] * 2,
        out_specs=[pl.BlockSpec(memory_space=pl.ANY)] * 2,
        scratch_shapes=[
            pltpu.SemaphoreType.DMA((send_count,)),
            pltpu.SemaphoreType.DMA((2, size)),
            pltpu.SemaphoreType.DMA((2,)),
        ],
        compiler_params=pltpu.CompilerParams(collective_id=0, has_side_effects=True),
    )(first, second)
    return [x.reshape(-1, x.shape[-1]) for x in outs]


def local(
    tokens,
    cotangent,
    gate_probs,
    expert_ids,
    gate_up,
    down_weight,
    gate_up_moment,
    gate_up_second,
    down_moment,
    down_second,
):
    expert_count = lax.axis_size("expert")
    model_width = tokens.shape[1]
    me = lax.axis_index("expert")
    experts = jnp.arange(expert_count, dtype=jnp.int32)
    dense = jnp.sum(
        jnp.where(expert_ids[:, :, None] == experts, gate_probs[:, :, None], 0.0), axis=1
    )
    high = dense.astype(jnp.bfloat16)
    low = (dense - high.astype(jnp.float32)).astype(jnp.bfloat16)
    pad = -2 * expert_count % 128
    side = jnp.concatenate([high, low, jnp.zeros((tokens.shape[0], pad), jnp.bfloat16)], axis=1)
    all_tokens, gathered = gather_pair(tokens, jnp.concatenate([cotangent, side], axis=1))
    all_cotangent = gathered[:, :model_width]
    weight = sum(
        lax.dynamic_slice_in_dim(gathered, model_width + part * expert_count + me, 1, 1).astype(
            jnp.float32
        )
        for part in range(2)
    )
    weight_pair = gate_up[0]
    weight_down = down_weight[0]
    hidden_count = weight_down.shape[0]
    projected = contract(all_tokens, weight_pair, ((1,), (0,)))
    gate_part = projected[:, :hidden_count]
    up_part = projected[:, hidden_count:]
    sigmoid_gate = jax.nn.sigmoid(gate_part)
    activated = gate_part * sigmoid_gate
    hidden_act = (weight * activated * up_part).astype(jnp.bfloat16)
    hidden_grad = weight * contract(all_cotangent, weight_down, ((1,), (1,)))
    slope = sigmoid_gate * (1.0 + gate_part * (1.0 - sigmoid_gate))
    pair_grad = jnp.concatenate(
        [hidden_grad * up_part * slope, hidden_grad * activated], axis=1
    ).astype(jnp.bfloat16)
    row_grads = contract(pair_grad, weight_pair, ((1,), (1,))).astype(jnp.bfloat16)
    row_grads, pair_grad = lax.optimization_barrier((row_grads, pair_grad))
    token_grad = lax.psum_scatter(row_grads, "expert", scatter_dimension=0, tiled=True)
    grad_pair = contract(all_tokens, pair_grad, ((0,), (0,)))
    sum_pair = group_reduce(grad_pair, 0)[None]
    grad_down = contract(hidden_act, all_cotangent, ((0,), (0,)))
    sum_down = group_reduce(grad_down, 1)[None]
    group_index = lax.axis_index("group")
    share_rows = model_width // lax.axis_size("group")
    own_pair = lax.dynamic_slice_in_dim(gate_up, group_index * share_rows, share_rows, 1)
    own_down = lax.dynamic_slice_in_dim(down_weight, group_index * share_rows, share_rows, 2)
    new_pair, first_pair, second_pair = adam_update(
        own_pair, sum_pair, gate_up_moment, gate_up_second
    )
    new_down, first_down, second_down = adam_update(
        own_down, sum_down, down_moment, down_second
    )
    full_pair = group_gather(new_pair, 1)
    full_down = group_gather(new_down, 2)
    return (token_grad, full_pair, full_down, first_pair, second_pair, first_down, second_down)


def solution(mesh):
    placed = (
        P(("group", "expert"), None),
        P(("group", "expert"), None),
        P(("group", "expert"), None),
        P(("group", "expert"), None),
        P("expert", None, None),
        P("expert", None, None),
        P("expert", "group", None),
        P("expert", "group", None),
        P("expert", None, "group"),
        P("expert", None, "group"),
    )
    return jax.shard_map(
        local,
        mesh=mesh,
        in_specs=placed,
        out_specs=(
            P(("group", "expert"), None),
            P("expert", None, None),
            P("expert", None, None),
            P("expert", "group", None),
            P("expert", "group", None),
            P("expert", None, "group"),
            P("expert", None, "group"),
        ),
        check_vma=False,
    )
```
